128 devices in a mesh: leaf: 32 (over x, y, core), sub: 4 (over z).
Axes of the slice: x: 4, y: 4, z: 4, core: 2. Of those that a mesh axis runs over, the one named last changes fastest.
Arguments:
- densities: bfloat16 [16, 524288], P(None, ('leaf', 'sub')), may hold values from -6 to 6
- basis: bfloat16 [2048, 64, 256], P(('leaf', 'sub')), may hold values from -0.375 to 0.375
- near_blocks: bfloat16 [2048, 2048, 256], P(('leaf', 'sub')), may hold values from -0.125 to 0.125
- near_source: int32 [2048, 8], P(('leaf', 'sub')), may hold values from 0 to 2047, as said below
- near_valid: int32 [2048, 8], P(('leaf', 'sub')), may hold values from 0 to 1
- leaf_coupling: bfloat16 [2048, 64, 2048], P(('leaf', 'sub')), may hold values from -0.125 to 0.125
- leaf_source: int32 [2048, 32], P(('leaf', 'sub')), may hold values from 0 to 2047, as said below
- leaf_valid: int32 [2048, 32], P(('leaf', 'sub')), may hold values from 0 to 1
- parent_transfer: bfloat16 [256, 64, 512], P(('leaf', 'sub')), may hold values from -0.4375 to 0.4375
- parent_coupling: bfloat16 [256, 64, 2048], P(('leaf', 'sub')), may hold values from -0.125 to 0.125
- parent_source: int32 [256, 32], P(('leaf', 'sub')), may hold values from 0 to 255
- parent_valid: int32 [256, 32], P(('leaf', 'sub')), may hold values 0 or 1
- grand_transfer: bfloat16 [32, 64, 512], replicated, may hold values from -0.4375 to 0.4375
- grand_coupling: bfloat16 [32, 64, 1024], P('leaf'), may hold values from -0.1875 to 0.1875
- grand_source: int32 [32, 16], P('leaf'), may hold values from 0 to 31
- grand_valid: int32 [32, 16], P('leaf'), may hold values 0 or 1
Outputs:
- potential: bfloat16 [16, 524288], P(None, ('leaf', 'sub'))
The draws below stay inside these ranges and needn't reach their ends.
Inputs may be any that keep to these rules, and one draw needn't show every extreme that they name: `leaf_source`: for the 16 leaves of one device (aligned blocks of rows), the slots with leaf_valid = 1 name leaves of any one aligned block of 16 leaves at most 8 times; this bound is reached in every draw. `near_source`: every near source leaf lies within 8 leaves of its target leaf in the curve order; both ends of the reach occur.
All inputs are finite; a program needn't handle non-finite values. No bound on the sum of `parent_valid` or of `grand_valid` on one device may be relied on, other than what follows from the above.
Results may differ from the reference program's by a relative error of at most 0.009.
Values may be sent and summed in bfloat16 or wider, within the bound.
No kernel may reach another device: no remote copies, remote signals or barrier semaphores. Data moves between devices by JAX's collectives and lax.ppermute only.
A program may use at most 128 MiB of HBM per device.

```python
import math
import jax
import jax.numpy as jnp
from jax import lax

B_DEV = 16
P_SIZE = 256
K = 64
R = 16
NEAR = 8
M0 = 32
M1 = 32
M2 = 16
LEAVES = 2048
POINTS = 524288
PARENTS = 256
GRAND = 32
CAP = 8
NW = 8


def coupling_plan(key):
    shards = LEAVES // B_DEV
    slot_total = B_DEV * M0
    busiest = jax.random.randint(jax.random.fold_in(key, 11), (), 0, shards)
    subkeys = jax.random.split(jax.random.fold_in(key, 12), shards)
    ranking = jax.vmap(lambda subkey: jax.random.permutation(subkey, slot_total))(subkeys)
    forced = ranking < CAP
    peer_index = jax.random.randint(jax.random.fold_in(key, 13), (shards, slot_total), 0, shards - 1)
    peer_index = jnp.where(peer_index >= busiest, peer_index + 1, peer_index)
    peer_index = jnp.where(forced, busiest, peer_index)
    kept_slots = (jax.random.randint(jax.random.fold_in(key, 14), (shards, slot_total), 0, 10) < 9) | forced
    onehot = ((peer_index[:, :, None] == jnp.arange(shards, dtype=jnp.int32)[None, None, :]) & kept_slots[:, :, None]).astype(jnp.int32)
    before = jnp.cumsum(onehot, axis=1) - onehot
    arrival = jnp.sum(before * onehot, axis=2)
    kept_slots = kept_slots & (arrival < CAP)
    member_leaf = jax.random.randint(jax.random.fold_in(key, 15), (shards, slot_total), 0, B_DEV)
    source = (peer_index * B_DEV + member_leaf).reshape(LEAVES, M0).astype(jnp.int32)
    return (source, kept_slots.reshape(LEAVES, M0).astype(jnp.int32))


def near_plan(key):
    target = jnp.arange(LEAVES, dtype=jnp.int32)[:, None]
    offset = jax.random.randint(jax.random.fold_in(key, 21), (LEAVES, NEAR), -NW, NW + 1)
    chosen = jax.random.randint(jax.random.fold_in(key, 22), (LEAVES, 1), 0, NEAR)
    edge_offset = jnp.where(target % 2 == 0, NW, -NW)
    edge_slot = jnp.arange(NEAR, dtype=jnp.int32)[None, :] == chosen
    offset = jnp.where(edge_slot, edge_offset, offset)
    source = jnp.clip(target + offset, 0, LEAVES - 1).astype(jnp.int32)
    valid_slots = (jax.random.randint(jax.random.fold_in(key, 23), (LEAVES, NEAR), 0, 4) < 3) | edge_slot
    return (source, valid_slots.astype(jnp.int32))


def draw_leaf_source(key, part):
    source, valid_slots = coupling_plan(key)
    return source


def draw_leaf_valid(key, part):
    source, valid_slots = coupling_plan(key)
    return valid_slots


def draw_near_source(key, part):
    source, valid_slots = near_plan(key)
    return source


def draw_near_valid(key, part):
    source, valid_slots = near_plan(key)
    return valid_slots


def plant(entries, rng, smallest, high):
    spot = [jax.random.randint(jax.random.fold_in(rng, axis), (), 0, length) for axis, length in enumerate(entries.shape)]
    main_axis = entries.shape.index(max(entries.shape))
    neighbour = spot[:main_axis] + [(spot[main_axis] + 1) % entries.shape[main_axis]] + spot[main_axis + 1:]
    return entries.at[tuple(spot)].set(smallest).at[tuple(neighbour)].set(high)


def block_levels(key, shape, cuts, low, top_value):
    gain, own = 1.0, jax.random.fold_in(key, 6)
    for position, parts in cuts:
        draws = jnp.exp(jax.random.uniform(jax.random.fold_in(own, position), (parts,), jnp.float32, low / len(cuts), top_value / len(cuts)))
        gain = gain * jnp.repeat(draws, shape[position] // parts).reshape([-1 if axis == position else 1 for axis in range(len(shape))])
    return gain


def scatter_about(own_key, extent, spread, limit, cuts=(), held_as=jnp.bfloat16):
    values = spread * jax.random.normal(own_key, extent, jnp.float32)
    if cuts:
        values = values * block_levels(own_key, extent, cuts, -0.22, 0.18)
    return jnp.clip(values, -limit, limit).astype(held_as)


def setup_inputs(seed: int = 0) -> dict:
    splits = jax.random.split(jax.random.key(seed), 17)
    densities = scatter_about(splits[0], (R, POINTS), 1.0, 6.0, ((1, 128),))
    basis = scatter_about(splits[1], (LEAVES, K, P_SIZE), P_SIZE ** -0.5, 0.375, ((0, 128),))
    near_blocks = scatter_about(splits[2], (LEAVES, NEAR * P_SIZE, P_SIZE), (NEAR * P_SIZE) ** -0.5, 0.125, ((0, 128),))
    near_source = draw_near_source(jax.random.fold_in(splits[16], 71), 0)
    near_valid = draw_near_valid(jax.random.fold_in(splits[16], 71), 0)
    leaf_coupling = scatter_about(splits[5], (LEAVES, K, M0 * K), (M0 * K) ** -0.5, 0.125, ((0, 128),))
    leaf_source = draw_leaf_source(jax.random.fold_in(splits[16], 71), 0)
    leaf_valid = draw_leaf_valid(jax.random.fold_in(splits[16], 71), 0)
    parent_transfer = scatter_about(splits[8], (PARENTS, K, 8 * K), (3 * K) ** -0.5, 0.4375, ((0, 128),))
    parent_coupling = scatter_about(splits[9], (PARENTS, K, M1 * K), (M1 * K) ** -0.5, 0.125, ((0, 128),))
    parent_source = plant(jax.random.randint(splits[10], (PARENTS, M1), 0, PARENTS), jax.random.fold_in(splits[10], 1), 0, PARENTS - 1).astype(jnp.int32)
    parent_valid = plant((jax.random.randint(splits[11], (PARENTS, M1), 0, 4) < 3).astype(jnp.int32), jax.random.fold_in(splits[11], 1), 0, 1)
    grand_transfer = scatter_about(splits[12], (GRAND, K, 8 * K), (3 * K) ** -0.5, 0.4375)
    grand_coupling = scatter_about(splits[13], (GRAND, K, M2 * K), (M2 * K) ** -0.5, 0.1875, ((0, 32),))
    grand_source = plant(jax.random.randint(splits[14], (GRAND, M2), 0, GRAND), jax.random.fold_in(splits[14], 1), 0, GRAND - 1).astype(jnp.int32)
    grand_valid = plant((jax.random.randint(splits[15], (GRAND, M2), 0, 4) < 3).astype(jnp.int32), jax.random.fold_in(splits[15], 1), 0, 1)
    return {"densities": densities, "basis": basis, "near_blocks": near_blocks, "near_source": near_source, "near_valid": near_valid, "leaf_coupling": leaf_coupling, "leaf_source": leaf_source, "leaf_valid": leaf_valid, "parent_transfer": parent_transfer, "parent_coupling": parent_coupling, "parent_source": parent_source, "parent_valid": parent_valid, "grand_transfer": grand_transfer, "grand_coupling": grand_coupling, "grand_source": grand_source, "grand_valid": grand_valid}


def blockwise(function, operands, total):
    group_size = math.gcd(total, 64)
    shaped = tuple(operand.reshape((total // group_size, group_size) + operand.shape[1:]) for operand in operands)
    result = lax.map(function, shaped)
    return result.reshape((total,) + result.shape[2:])


def couple(coefficients, source, valid_slots, blocks):
    rank_width = coefficients.shape[-1]

    def one_block(operands):
        block_source, block_valid, block_moves = operands
        picked = jnp.take(coefficients, block_source, axis=0)
        picked = jnp.where(block_valid[:, :, None, None] == 1, picked, jnp.zeros((), coefficients.dtype))
        coupling_view = block_moves.reshape(block_moves.shape[0], rank_width, block_source.shape[1], rank_width)
        return jnp.einsum('tjrb,tajb->tra', picked.astype(jnp.float32), coupling_view.astype(jnp.float32))

    return blockwise(one_block, (source, valid_slots, blocks), source.shape[0])


def reference(densities, basis, near_blocks, near_source, near_valid, leaf_coupling, leaf_source, leaf_valid, parent_transfer, parent_coupling, parent_source, parent_valid, grand_transfer, grand_coupling, grand_source, grand_valid):
    right_sides = densities.shape[0]
    leaves, rank_width, leaf_width = basis.shape
    parents = leaves // 8
    grands = parents // 8
    blocked = densities.reshape(right_sides, leaves, leaf_width)
    upward = jnp.einsum('rtp,tkp->trk', blocked.astype(jnp.float32), basis.astype(jnp.float32)).astype(jnp.bfloat16)
    children = upward.reshape(parents, 8, right_sides, rank_width)
    parent_up = jnp.einsum('pcrb,pkcb->prk', children.astype(jnp.float32), parent_transfer.reshape(parents, rank_width, 8, rank_width).astype(jnp.float32)).astype(jnp.bfloat16)
    grand_children = parent_up.reshape(grands, 8, right_sides, rank_width)
    grand_up = jnp.einsum('gcrb,gkcb->grk', grand_children.astype(jnp.float32), grand_transfer.reshape(grands, rank_width, 8, rank_width).astype(jnp.float32)).astype(jnp.bfloat16)
    leaf_far = couple(upward, leaf_source, leaf_valid, leaf_coupling)
    parent_far = couple(parent_up, parent_source, parent_valid, parent_coupling)
    grand_total = couple(grand_up, grand_source, grand_valid, grand_coupling).astype(jnp.bfloat16)
    down_two = jnp.einsum('grk,gkm->grm', grand_total.astype(jnp.float32), grand_transfer.astype(jnp.float32))
    down_two = down_two.reshape(grands, right_sides, 8, rank_width).transpose(0, 2, 1, 3).reshape(parents, right_sides, rank_width)
    parent_total = (parent_far + down_two).astype(jnp.bfloat16)
    down_one = jnp.einsum('prk,pkm->prm', parent_total.astype(jnp.float32), parent_transfer.astype(jnp.float32))
    down_one = down_one.reshape(parents, right_sides, 8, rank_width).transpose(0, 2, 1, 3).reshape(leaves, right_sides, rank_width)
    leaf_total = (leaf_far + down_one).astype(jnp.bfloat16)

    def near_block(operands):
        block_source, block_valid, block_dense, block_basis, block_total = operands
        picked = jnp.take(blocked, block_source, axis=1)
        picked = jnp.where(block_valid[None, :, :, None] == 1, picked, jnp.zeros((), blocked.dtype))
        picked = picked.reshape(right_sides, block_source.shape[0], -1)
        near_field = jnp.einsum('rtm,tmq->trq', picked.astype(jnp.float32), block_dense.astype(jnp.float32))
        far_field = jnp.einsum('trk,tkq->trq', block_total.astype(jnp.float32), block_basis.astype(jnp.float32))
        return far_field + near_field

    summed = blockwise(near_block, (near_source, near_valid, near_blocks, basis, leaf_total), leaves)
    return summed.astype(jnp.bfloat16).transpose(1, 0, 2).reshape(right_sides, leaves * leaf_width)
```

```python
import jax
import jax.numpy as jnp
from jax import lax
from jax.experimental import pallas as pl
from jax.experimental.pallas import tpu as pltpu
from jax.sharding import Mesh, PartitionSpec as P

AXES = ("x", "y", "c", "z")
BF16, F32 = jnp.bfloat16, jnp.float32
TILES = 9
VMEM_LIMIT = 50 * 1024 * 1024


def flat_index(x, y, c, z):
    return ((x * 4 + y) * 2 + c) * 4 + z


def pairs_of(move):
    return [
        (flat_index(x, y, c, z), flat_index(*move(x, y, c, z)))
        for x in range(4)
        for y in range(4)
        for c in range(2)
        for z in range(4)
    ]


def dot_t(a, b):
    return lax.dot_general(a, b, (((1,), (1,)), ((), ())), preferred_element_type=F32)


def dot(a, b):
    return lax.dot_general(a, b, (((1,), (0,)), ((), ())), preferred_element_type=F32)


def up_kernel(dens_ref, basis_ref, pt_ref, out_ref):
    tiles = []
    for i in range(8):
        pair = [
            dot_t(dens_ref[:, t * 256 : (t + 1) * 256], basis_ref[t]).astype(BF16)
            for t in (2 * i, 2 * i + 1)
        ]
        tile = jnp.concatenate(pair, axis=1)
        out_ref[i] = tile
        tiles.append(tile)
    pair = [
        dot_t(jnp.concatenate(tiles[4 * p : 4 * p + 4], axis=1), pt_ref[p]).astype(BF16)
        for p in range(2)
    ]
    out_ref[8] = jnp.concatenate(pair, axis=1)


def near_kernel(idx_ref, left_ref, dens_ref, right_ref, blocks_ref, out_ref, padded):
    t = pl.program_id(0)

    @pl.when(t == 0)
    def _():
        for i in range(8):
            padded[i] = left_ref[:, i * 256 : (i + 1) * 256]
            padded[24 + i] = right_ref[:, i * 256 : (i + 1) * 256]
        for i in range(16):
            padded[8 + i] = dens_ref[:, i * 256 : (i + 1) * 256]
        padded[32] = jnp.zeros((16, 256), BF16)

    picked = jnp.concatenate([padded[idx_ref[t * 8 + j]] for j in range(8)], axis=1)
    out_ref[...] = dot(picked, blocks_ref[0])


def down_kernel(
    leaf_ref, parent_ref, grand_ref, own_ref,
    p0, p1, p2, p3, p4, p5, p6, p7,
    lc_hbm, pc_hbm, gc_hbm, gt_hbm, pt_ref, basis_ref, near_ref,
    out_ref,
    table, lc, pc, gc, gt, picked, leaf_far, sems,
):
    pieces = (p0, p1, p2, p3, p4, p5, p6, p7)
    copies = [
        pltpu.make_async_copy(p, table.at[pl.ds(k * 144, 144)], sems.at[k])
        for k, p in enumerate(pieces)
    ]
    others = [
        pltpu.make_async_copy(a, b, sems.at[8 + k])
        for k, (a, b) in enumerate(((gt_hbm, gt), (gc_hbm, gc), (pc_hbm, pc), (lc_hbm, lc)))
    ]
    for copy in copies + others:
        copy.start()
    table[1152] = jnp.zeros((16, 128), BF16)
    low = lax.broadcasted_iota(jnp.int32, (16, 128), 1) < 64
    for copy in copies:
        copy.wait()

    def pair_tile(ref, at):
        halves = []
        for k in range(2):
            code = ref[at + k]
            tile = table[code // 2].astype(F32)
            halves.append(pltpu.roll(tile, (code % 2) * 64, 1))
        return jnp.where(low, halves[0], halves[1]).astype(BF16)

    others[0].wait()
    ups = []
    for j in range(16):
        children = jnp.concatenate([table[grand_ref[j * 5 + 1 + z]] for z in range(4)], axis=1)
        ups.append(dot_t(children, gt[grand_ref[j * 5]]).astype(BF16))
    others[1].wait()
    grand_total = dot_t(jnp.concatenate(ups, axis=1), gc[0]).astype(BF16)
    down_two = dot(grand_total, gt[own_ref[0], :, pl.ds(pl.multiple_of(own_ref[1] * 128, 128), 128)])

    others[2].wait()
    down_one = []
    for p in range(2):
        coefs = jnp.concatenate([pair_tile(parent_ref, p * 32 + 2 * i) for i in range(16)], axis=1)
        far = dot_t(coefs, pc[p])
        total = (far + down_two[:, p * 64 : (p + 1) * 64]).astype(BF16)
        down_one.append(dot(total, pt_ref[p]))

    def gather(t, carry):
        for i in range(16):
            picked[t, :, i * 128 : (i + 1) * 128] = pair_tile(leaf_ref, t * 32 + 2 * i)
        return carry

    lax.fori_loop(0, 16, gather, 0)
    others[3].wait()
    for t in range(16):
        far = dot_t(picked[t], lc[t])
        total = (far + down_one[t // 8][:, (t % 8) * 64 : (t % 8 + 1) * 64]).astype(BF16)
        cols = slice(t * 256, (t + 1) * 256)
        out_ref[:, cols] = (dot(total, basis_ref[t]) + near_ref[:, cols]).astype(BF16)


def gather_z(v):
    step = lax.ppermute(v, "z", [(i, i ^ 1) for i in range(4)])
    v = jnp.concatenate([v, step], axis=0)
    step = lax.ppermute(v, "z", [(i, i ^ 3) for i in range(4)])
    return jnp.concatenate([v, step], axis=0)


def shift_plane(v, k, y_core):
    return lax.ppermute(
        v,
        AXES,
        pairs_of(
            lambda x, y, c, z: (x, (y + k) % 4, c, z) if c == y_core else ((x + k) % 4, y, c, z)
        ),
    )


def body(
    densities, basis, near_blocks, near_source, near_valid, leaf_coupling, leaf_source, leaf_valid,
    parent_transfer, parent_coupling, parent_source, parent_valid, grand_transfer, grand_coupling,
    grand_source, grand_valid,
):
    mx, my, mc, mz = (lax.axis_index(a) for a in AXES)
    me = lax.axis_index(AXES)

    def block_tile(device):
        z, c, y, x = device % 4, device // 4 % 2, device // 8 % 4, device // 32
        w = z ^ mz
        kz = w ^ (w >> 1)
        ky, kx = (my - y) % 4, (mx - x) % 4
        block = jnp.where(c == 0, kx * 16 + ky * 4, ky * 16 + kx * 4) + kz
        return (jnp.where(c == mc, 0, 64) + block) * TILES

    slot = jnp.arange(32, dtype=jnp.int32)
    leaf_code = (block_tile(leaf_source // 16) + leaf_source % 16 // 2) * 2 + (leaf_source + slot) % 2
    leaf_code = jnp.where(leaf_valid == 1, leaf_code, 1152 * 2).reshape(-1)
    parent_code = (block_tile(parent_source // 2) + 8) * 2 + (parent_source + slot) % 2
    parent_code = jnp.where(parent_valid == 1, parent_code, 1152 * 2).reshape(-1)
    grand_tiles = block_tile(grand_source[0][:, None] * 4 + jnp.arange(4, dtype=jnp.int32)) + 8
    grand_tiles = jnp.where(grand_valid[0][:, None] == 1, grand_tiles, 1152)
    grand_code = jnp.concatenate([grand_source[0][:, None], grand_tiles], axis=1).reshape(-1)
    own = jnp.stack([me // 4, mz]).astype(jnp.int32)
    near_code = jnp.where(near_valid == 1, near_source - (me * 16 - 8), 32).reshape(-1)

    coefs = pl.pallas_call(
        up_kernel,
        out_shape=jax.ShapeDtypeStruct((TILES, 16, 128), BF16),
        compiler_params=pltpu.CompilerParams(vmem_limit_bytes=VMEM_LIMIT),
        name="upward",
    )(densities, basis, parent_transfer)

    coefs = gather_z(coefs)
    coefs = jnp.concatenate([coefs] + [shift_plane(coefs, k, 0) for k in (1, 2, 3)], axis=0)
    pieces = [coefs] + [shift_plane(coefs, k, 1) for k in (1, 2, 3)]
    other = [lax.ppermute(p, "c", [(0, 1), (1, 0)]) for p in pieces]

    left = lax.ppermute(densities[:, 2048:], AXES, [(i, i + 1) for i in range(127)])
    right = lax.ppermute(densities[:, :2048], AXES, [(i + 1, i) for i in range(127)])
    near = pl.pallas_call(
        near_kernel,
        out_shape=jax.ShapeDtypeStruct((16, 4096), F32),
        grid_spec=pltpu.PrefetchScalarGridSpec(
            num_scalar_prefetch=1,
            grid=(16,),
            in_specs=[
                pl.BlockSpec((16, 2048), lambda t, i: (0, 0)),
                pl.BlockSpec((16, 4096), lambda t, i: (0, 0)),
                pl.BlockSpec((16, 2048), lambda t, i: (0, 0)),
                pl.BlockSpec((1, 2048, 256), lambda t, i: (t, 0, 0)),
            ],
            out_specs=pl.BlockSpec((16, 256), lambda t, i: (0, t)),
            scratch_shapes=[pltpu.VMEM((33, 16, 256), BF16)],
        ),
        compiler_params=pltpu.CompilerParams(vmem_limit_bytes=VMEM_LIMIT),
        cost_estimate=pl.CostEstimate(
            flops=2 * 16 * 16 * 2048 * 256, bytes_accessed=17_500_000, transcendentals=0
        ),
        name="near",
    )(near_code, left, densities, right, near_blocks)

    anywhere = pl.BlockSpec(memory_space=pl.ANY)
    vmem = pl.BlockSpec(memory_space=pltpu.VMEM)
    smem = pl.BlockSpec(memory_space=pltpu.SMEM)
    return pl.pallas_call(
        down_kernel,
        out_shape=jax.ShapeDtypeStruct((16, 4096), BF16),
        in_specs=[smem] * 4 + [anywhere] * 12 + [vmem] * 3,
        out_specs=vmem,
        scratch_shapes=[
            pltpu.VMEM((1153, 16, 128), BF16),
            pltpu.VMEM((16, 64, 2048), BF16),
            pltpu.VMEM((2, 64, 2048), BF16),
            pltpu.VMEM((1, 64, 1024), BF16),
            pltpu.VMEM((32, 64, 512), BF16),
            pltpu.VMEM((16, 16, 2048), BF16),
            pltpu.VMEM((16, 16, 64), F32),
            pltpu.SemaphoreType.DMA((12,)),
        ],
        compiler_params=pltpu.CompilerParams(vmem_limit_bytes=VMEM_LIMIT),
        name="downward",
    )(
        leaf_code, parent_code, grand_code, own, *pieces, *other,
        leaf_coupling, parent_coupling, grand_coupling, grand_transfer, parent_transfer, basis, near,
    )


def solution(mesh):
    grid = Mesh(mesh.devices.reshape(4, 4, 2, 4), AXES)
    leaf, both = ("x", "y", "c"), AXES
    row, cube = P(both, None), P(both, None, None)
    return jax.shard_map(
        body,
        mesh=grid,
        in_specs=(
            P(None, both), cube, cube, row, row, cube, row, row, cube, cube, row, row, P(),
            P(leaf, None, None), P(leaf, None), P(leaf, None),
        ),
        out_specs=P(None, both),
        check_vma=False,
    )
```

```python
import functools

import jax
import jax.numpy as jnp
from jax import lax
from jax.experimental import pallas as pl
from jax.experimental.pallas import tpu as pltpu
from jax.sharding import Mesh, PartitionSpec as P

AXES = ("x", "y", "c", "z")
BF16, F32 = jnp.bfloat16, jnp.float32
TILES = 9
HALF = 8 * TILES
UP_VMEM, CODE_VMEM, STAGE_VMEM, NEAR_VMEM = 56_500_000, 65_000_000, 1 << 20, 40_000_000
AHEAD = 4
DOWN_VMEM = 20 * 1024 * 1024


def flat_index(x, y, c, z):
    return ((x * 4 + y) * 2 + c) * 4 + z


def pairs_of(move):
    return [
        (flat_index(x, y, c, z), flat_index(*move(x, y, c, z)))
        for x in range(4)
        for y in range(4)
        for c in range(2)
        for z in range(4)
    ]


def dot_t(a, b):
    return lax.dot_general(a, b, (((1,), (1,)), ((), ())), preferred_element_type=F32)


def dot(a, b):
    return lax.dot_general(a, b, (((1,), (0,)), ((), ())), preferred_element_type=F32)


def up_kernel(
    dens_hbm, basis_hbm, pt_hbm, out_ref, inner_ref, outer_ref, dens_ref, basis_ref, pt_ref, sems
):
    copies = [
        pltpu.make_async_copy(a, b, sems.at[k])
        for k, (a, b) in enumerate(
            ((dens_hbm, dens_ref), (basis_hbm, basis_ref), (pt_hbm, pt_ref))
        )
    ]
    for copy in copies:
        copy.start()
    for copy in copies:
        copy.wait()
    even = lax.axis_index("z") % 2 == 0
    for i in range(8):
        cols = slice(i * 256, (i + 1) * 256)
        head, tail = dens_ref[:, cols], dens_ref[:, 2048 + i * 256 : 2304 + i * 256]
        inner_ref[:, cols] = jnp.where(even, tail, head)
        outer_ref[:, cols] = jnp.where(even, head, tail)
    tiles = []
    for i in range(8):
        pair = [
            dot_t(dens_ref[:, t * 256 : (t + 1) * 256], basis_ref[t]).astype(BF16)
            for t in (2 * i, 2 * i + 1)
        ]
        tile = jnp.concatenate(pair, axis=1)
        out_ref[i] = tile
        tiles.append(tile)
    pair = [
        dot_t(jnp.concatenate(tiles[4 * p : 4 * p + 4], axis=1), pt_ref[p]).astype(BF16)
        for p in range(2)
    ]
    out_ref[8] = jnp.concatenate(pair, axis=1)


def code_kernel(
    ns_ref, nv_ref, ls_ref, lv_ref, ps_ref, pv_ref, gs_ref, gv_ref,
    near_ref, leaf_ref, parent_ref, grand_ref,
):
    mx, my, mc, mz = (lax.axis_index(a) for a in AXES)
    me = flat_index(mx, my, mc, mz)

    def block_tile(device):
        z, c, y, x = device & 3, (device >> 2) & 1, (device >> 3) & 3, device >> 5
        w = z ^ mz
        kz = w ^ (w >> 1)
        ky, kx = (my - y) & 3, (mx - x) & 3
        near_step, far_step = jnp.where(c == 0, ky, kx), jnp.where(c == 0, kx, ky)
        half = near_step >> 1
        unit = jnp.where(far_step == 1, 2 + 2 * half, jnp.where(far_step == 3, 5 - 2 * half, 6 + half))
        unit = jnp.where(far_step == 0, half, unit) + jnp.where(c == mc, 0, 8)
        return unit * HALF + ((near_step & 1) * 4 + kz) * TILES

    def code(tile, source, valid):
        flip = (source + lax.broadcasted_iota(jnp.int32, source.shape, 1)) & 1
        return tile * 4 + valid * 2 + flip

    near_ref[...] = jnp.where(nv_ref[...] == 1, ns_ref[...] - (me * 16 - 8), 32)
    ls = ls_ref[...]
    leaf_ref[...] = code(block_tile(ls >> 4) + ((ls >> 1) & 7), ls, lv_ref[...])
    ps = ps_ref[...]
    parent_ref[...] = code(block_tile(ps >> 1) + 8, ps, pv_ref[...])
    gs = gs_ref[...]
    grand_ref[0:1] = gs
    for z in range(4):
        grand_ref[1 + z : 2 + z] = block_tile(gs * 4 + z) + 8
    grand_ref[5:6] = gv_ref[...]


def stage_kernel(code_ref, dens_ref, out_ref, tiles_ref):
    out_ref[...] = code_ref[...]
    for i in range(16):
        tiles_ref[i] = dens_ref[:, i * 256 : (i + 1) * 256]


def near_kernel(turn, idx_ref, halo_ref, tiles_ref, blocks_hbm, out_ref, padded, blocks, sems):
    half = (lax.axis_index("z") + 1 + turn) & 1
    copies = [
        pltpu.make_async_copy(blocks_hbm.at[half * 8 + t], blocks.at[t], sems.at[t])
        for t in range(8)
    ]
    for copy in copies[:AHEAD]:
        copy.start()
    for i in range(8):
        padded[24 * half + i] = halo_ref[:, i * 256 : (i + 1) * 256]
    for i in range(16):
        padded[8 + i] = tiles_ref[i]
    padded[32] = jnp.zeros((16, 256), BF16)
    for t in range(8):
        if t + AHEAD < 8:
            copies[t + AHEAD].start()
        picked = jnp.concatenate([padded[idx_ref[j, half * 8 + t]] for j in range(8)], axis=1)
        copies[t].wait()
        out_ref[:, t * 256 : (t + 1) * 256] = dot(picked, blocks[t])


def down_kernel(
    leaf_ref, parent_ref, grand_ref, own_ref,
    table, lc, pc, gc, gt, pt_ref, basis_ref, near0_ref, near1_ref,
    out_ref,
):
    first = lax.axis_index("z") % 2 == 1
    second = jnp.logical_not(first)
    low = lax.broadcasted_iota(jnp.int32, (16, 128), 1) < 64
    zero = jnp.zeros((16, 128), BF16)

    def pair_tile(ref, t, j):
        first, second = ref[t, j], ref[t, j + 1]
        a, b = table[first >> 2], table[second >> 2]
        straight = jnp.where(low, a, b)
        crossed = pltpu.roll(jnp.where(low, b, a), 64, 1)
        kind = jnp.where(low, first, second) & 3
        return jnp.where(kind == 2, straight, jnp.where(kind == 3, crossed, zero))

    ups = []
    for j in range(16):
        children = jnp.concatenate([table[grand_ref[1 + z, j]] for z in range(4)], axis=1)
        up = dot_t(children, gt[grand_ref[0, j]])
        ups.append(jnp.where(grand_ref[5, j] == 1, up, 0.0).astype(BF16))
    grand_total = dot_t(jnp.concatenate(ups, axis=1), gc[0]).astype(BF16)
    down_two = dot(grand_total, gt[own_ref[0], :, pl.ds(pl.multiple_of(own_ref[1] * 128, 128), 128)])

    down_one = []
    for p in range(2):
        coefs = jnp.concatenate([pair_tile(parent_ref, p, 2 * i) for i in range(16)], axis=1)
        far = dot_t(coefs, pc[p])
        total = (far + down_two[:, p * 64 : (p + 1) * 64]).astype(BF16)
        down_one.append(dot(total, pt_ref[p]))

    for g in range(4):
        coefs = jnp.concatenate(
            [
                jnp.concatenate([pair_tile(leaf_ref, t, 2 * i) for i in range(16)], axis=1)
                for t in range(4 * g, 4 * g + 4)
            ],
            axis=0,
        )
        far = dot_t(coefs, lc[4 * g : 4 * g + 4].reshape(256, 2048))
        for k in range(4):
            t = 4 * g + k
            total = far[k * 16 : (k + 1) * 16, k * 64 : (k + 1) * 64]
            total = total + down_one[t // 8][:, (t % 8) * 64 : (t % 8 + 1) * 64]
            cols = slice(t * 256, (t + 1) * 256)
            here = slice((t % 8) * 256, (t % 8 + 1) * 256)
            near = jnp.where(second if t < 8 else first, near1_ref[:, here], near0_ref[:, here])
            out_ref[:, cols] = (dot(total.astype(BF16), basis_ref[t]) + near).astype(BF16)


def shift_plane(v, k, y_core):
    return lax.ppermute(
        v,
        AXES,
        pairs_of(
            lambda x, y, c, z: (x, (y + k) % 4, c, z) if c == y_core else ((x + k) % 4, y, c, z)
        ),
    )


def body(
    densities, basis, near_blocks, near_source, near_valid, leaf_coupling, leaf_source, leaf_valid,
    parent_transfer, parent_coupling, parent_source, parent_valid, grand_transfer, grand_coupling,
    grand_source, grand_valid,
):
    anywhere = pl.BlockSpec(memory_space=pl.ANY)
    vmem = pl.BlockSpec(memory_space=pltpu.VMEM)
    smem = pl.BlockSpec(memory_space=pltpu.SMEM)
    mz = lax.axis_index("z")
    own = jnp.stack([lax.axis_index(("x", "y", "c")), mz]).astype(jnp.int32)

    coefs, inner, outer = pl.pallas_call(
        up_kernel,
        out_shape=[
            jax.ShapeDtypeStruct((TILES, 16, 128), BF16),
            jax.ShapeDtypeStruct((16, 2048), BF16),
            jax.ShapeDtypeStruct((16, 2048), BF16),
        ],
        in_specs=[anywhere] * 3,
        out_specs=[vmem] * 3,
        scratch_shapes=[
            pltpu.VMEM((16, 4096), BF16),
            pltpu.VMEM((16, 64, 256), BF16),
            pltpu.VMEM((2, 64, 512), BF16),
            pltpu.SemaphoreType.DMA((3,)),
        ],
        compiler_params=pltpu.CompilerParams(vmem_limit_bytes=UP_VMEM),
        name="upward",
    )(densities, basis, parent_transfer)

    barrier = lax.optimization_barrier
    swap = [(0, 1), (1, 0)]

    def near_half(turn, halo, near_code):
        return pl.pallas_call(
            functools.partial(near_kernel, turn),
            out_shape=jax.ShapeDtypeStruct((16, 2048), F32),
            in_specs=[smem, vmem, vmem, anywhere],
            out_specs=vmem,
            scratch_shapes=[
                pltpu.VMEM((33, 16, 256), BF16),
                pltpu.VMEM((8, 2048, 256), BF16),
                pltpu.SemaphoreType.DMA((8,)),
            ],
            compiler_params=pltpu.CompilerParams(vmem_limit_bytes=NEAR_VMEM),
            cost_estimate=pl.CostEstimate(
                flops=16 * 16 * 2048 * 256, bytes_accessed=8_700_000, transcendentals=0
            ),
            name="near",
        )(near_code, halo, tiles, near_blocks)

    coefs, sources = barrier(
        (
            coefs,
            (near_source.T, near_valid.T, leaf_source, leaf_valid, parent_source, parent_valid,
             grand_source, grand_valid),
        )
    )
    step = lax.ppermute(coefs, "z", [(i, i ^ 1) for i in range(4)])
    inner = lax.ppermute(inner, AXES, [(i, i ^ 1) for i in range(128)])
    near_code, leaf_code, parent_code, grand_code = pl.pallas_call(
        code_kernel,
        out_shape=[
            jax.ShapeDtypeStruct(n, jnp.int32) for n in ((8, 16), (16, 32), (2, 32), (6, 16))
        ],
        compiler_params=pltpu.CompilerParams(vmem_limit_bytes=CODE_VMEM),
        name="codes",
    )(*sources)
    coefs, near_code, densities = barrier(
        (jnp.concatenate([coefs, step], axis=0), near_code, densities)
    )
    step = lax.ppermute(coefs, "z", [(i, i ^ 3) for i in range(4)])
    near_code, tiles = pl.pallas_call(
        stage_kernel,
        out_shape=[
            jax.ShapeDtypeStruct((8, 16), jnp.int32),
            jax.ShapeDtypeStruct((16, 16, 256), BF16),
        ],
        in_specs=[vmem] * 2,
        out_specs=[vmem] * 2,
        compiler_params=pltpu.CompilerParams(vmem_limit_bytes=STAGE_VMEM),
        name="stage",
    )(near_code, densities)
    coefs, inner, outer, near_code, tiles = barrier(
        (jnp.concatenate([coefs, step], axis=0), inner, outer, near_code, tiles)
    )

    steps = [shift_plane(coefs, k, 0) for k in (1, 2, 3)]
    near0 = near_half(0, inner, near_code)
    coefs, near0, outer = barrier((jnp.concatenate([coefs] + steps, axis=0), near0, outer))

    first, second = coefs[:HALF], coefs[HALF:]
    ahead1, back2 = shift_plane(first, 1, 1), shift_plane(second, 3, 1)
    outer = lax.ppermute(
        outer, AXES, [(i, i + 1) for i in range(1, 127, 2)] + [(i + 1, i) for i in range(1, 127, 2)]
    )
    ahead2, back1 = shift_plane(second, 1, 1), shift_plane(first, 3, 1)
    ahead1, back2, near_code = barrier((ahead1, back2, near_code))
    far1, far2 = shift_plane(ahead1, 1, 1), shift_plane(back2, 3, 1)
    near1 = near_half(1, outer, near_code)
    parts = [[coefs], [ahead1, back2], [ahead2, back1], [far1, far2]]
    other = [lax.ppermute(jnp.concatenate(p, axis=0), "c", swap) for p in parts]
    table = jnp.concatenate(sum(parts, []) + other, axis=0)

    return pl.pallas_call(
        down_kernel,
        out_shape=jax.ShapeDtypeStruct((16, 4096), BF16),
        in_specs=[smem] * 4 + [vmem] * 9,
        out_specs=vmem,
        compiler_params=pltpu.CompilerParams(vmem_limit_bytes=DOWN_VMEM),
        name="downward",
    )(
        leaf_code, parent_code, grand_code, own, table,
        leaf_coupling, parent_coupling, grand_coupling, grand_transfer, parent_transfer, basis,
        near0, near1,
    )


def solution(mesh):
    grid = Mesh(mesh.devices.reshape(4, 4, 2, 4), AXES)
    leaf, both = ("x", "y", "c"), AXES
    row, cube = P(both, None), P(both, None, None)
    return jax.shard_map(
        body,
        mesh=grid,
        in_specs=(
            P(None, both), cube, cube, row, row, cube, row, row, cube, cube, row, row, P(),
            P(leaf, None, None), P(leaf, None), P(leaf, None),
        ),
        out_specs=P(None, both),
        check_vma=False,
    )
```

```python
import functools

import jax
import jax.numpy as jnp
from jax import lax
from jax.experimental import pallas as pl
from jax.experimental.pallas import tpu as pltpu
from jax.sharding import Mesh, PartitionSpec as P

AXES = ("x", "y", "c", "z")
BF16, F32 = jnp.bfloat16, jnp.float32
TILES = 9
HALF = 8 * TILES
UP_VMEM, CODE_VMEM, STAGE_VMEM, NEAR_VMEM = 56_300_000, 65_000_000, 1 << 20, 40_000_000
AHEAD = 4
DOWN_VMEM = 20 * 1024 * 1024


def flat_index(x, y, c, z):
    return ((x * 4 + y) * 2 + c) * 4 + z


def pairs_of(move):
    return [
        (flat_index(x, y, c, z), flat_index(*move(x, y, c, z)))
        for x in range(4)
        for y in range(4)
        for c in range(2)
        for z in range(4)
    ]


def dot_t(a, b):
    return lax.dot_general(a, b, (((1,), (1,)), ((), ())), preferred_element_type=F32)


def dot(a, b):
    return lax.dot_general(a, b, (((1,), (0,)), ((), ())), preferred_element_type=F32)


def up_kernel(
    dens_hbm, basis_hbm, pt_hbm, out_ref, outer_ref, dens_ref, basis_ref, pt_ref, sems
):
    copies = [
        pltpu.make_async_copy(a, b, sems.at[k])
        for k, (a, b) in enumerate(
            ((dens_hbm, dens_ref), (basis_hbm, basis_ref), (pt_hbm, pt_ref))
        )
    ]
    for copy in copies:
        copy.start()
    for copy in copies:
        copy.wait()
    even = lax.axis_index("z") % 2 == 0
    for i in range(16):
        head, tail = (dens_ref[:, k * 128 : (k + 1) * 128] for k in (i, 16 + i))
        out_ref[TILES + i] = jnp.where(even, tail, head)
        outer_ref[i] = jnp.where(even, head, tail)
    tiles = []
    for i in range(8):
        pair = [
            dot_t(dens_ref[:, t * 256 : (t + 1) * 256], basis_ref[t]).astype(BF16)
            for t in (2 * i, 2 * i + 1)
        ]
        tile = jnp.concatenate(pair, axis=1)
        out_ref[i] = tile
        tiles.append(tile)
    pair = [
        dot_t(jnp.concatenate(tiles[4 * p : 4 * p + 4], axis=1), pt_ref[p]).astype(BF16)
        for p in range(2)
    ]
    out_ref[8] = jnp.concatenate(pair, axis=1)


def code_kernel(
    ns_ref, nv_ref, ls_ref, lv_ref, ps_ref, pv_ref, gs_ref, gv_ref,
    near_ref, leaf_ref, parent_ref, grand_ref,
):
    mx, my, mc, mz = (lax.axis_index(a) for a in AXES)
    me = flat_index(mx, my, mc, mz)

    def block_tile(device):
        z, c, y, x = device & 3, (device >> 2) & 1, (device >> 3) & 3, device >> 5
        w = z ^ mz
        kz = w ^ (w >> 1)
        ky, kx = (my - y) & 3, (mx - x) & 3
        near_step, far_step = jnp.where(c == 0, ky, kx), jnp.where(c == 0, kx, ky)
        half = near_step >> 1
        unit = jnp.where(far_step == 1, 2 + 2 * half, jnp.where(far_step == 3, 5 - 2 * half, 6 + half))
        unit = jnp.where(far_step == 0, half, unit) + jnp.where(c == mc, 0, 8)
        return unit * HALF + ((near_step & 1) * 4 + kz) * TILES

    def code(tile, source, valid):
        flip = (source + lax.broadcasted_iota(jnp.int32, source.shape, 1)) & 1
        return tile * 4 + valid * 2 + flip

    near_ref[...] = jnp.where(nv_ref[...] == 1, ns_ref[...] - (me * 16 - 8), 32)
    ls = ls_ref[...]
    leaf_ref[...] = code(block_tile(ls >> 4) + ((ls >> 1) & 7), ls, lv_ref[...])
    ps = ps_ref[...]
    parent_ref[...] = code(block_tile(ps >> 1) + 8, ps, pv_ref[...])
    gs = gs_ref[...]
    grand_ref[0:1] = gs
    for z in range(4):
        grand_ref[1 + z : 2 + z] = block_tile(gs * 4 + z) + 8
    grand_ref[5:6] = gv_ref[...]


def stage_kernel(code_ref, dens_ref, out_ref, tiles_ref):
    out_ref[...] = code_ref[...]
    for i in range(16):
        tiles_ref[i] = dens_ref[:, i * 256 : (i + 1) * 256]


def near_kernel(turn, skip, idx_ref, halo_ref, tiles_ref, blocks_hbm, out_ref, padded, blocks, sems):
    half = (lax.axis_index("z") + 1 + turn) & 1
    copies = [
        pltpu.make_async_copy(blocks_hbm.at[half * 8 + t], blocks.at[t], sems.at[t])
        for t in range(8)
    ]
    for copy in copies[:AHEAD]:
        copy.start()
    for i in range(8):
        pair = [halo_ref[skip + 2 * i + k] for k in range(2)]
        padded[24 * half + i] = jnp.concatenate(pair, axis=1)
    for i in range(16):
        padded[8 + i] = tiles_ref[i]
    padded[32] = jnp.zeros((16, 256), BF16)
    for t in range(8):
        if t + AHEAD < 8:
            copies[t + AHEAD].start()
        picked = jnp.concatenate([padded[idx_ref[j, half * 8 + t]] for j in range(8)], axis=1)
        copies[t].wait()
        out_ref[:, t * 256 : (t + 1) * 256] = dot(picked, blocks[t])


def down_kernel(
    leaf_ref, parent_ref, grand_ref, own_ref,
    table, lc, pc, gc, gt, pt_ref, basis_ref, near0_ref, near1_ref,
    out_ref,
):
    first = lax.axis_index("z") % 2 == 1
    second = jnp.logical_not(first)
    low = lax.broadcasted_iota(jnp.int32, (16, 128), 1) < 64
    zero = jnp.zeros((16, 128), BF16)

    def pair_tile(ref, t, j):
        first, second = ref[t, j], ref[t, j + 1]
        a, b = table[first >> 2], table[second >> 2]
        straight = jnp.where(low, a, b)
        crossed = pltpu.roll(jnp.where(low, b, a), 64, 1)
        kind = jnp.where(low, first, second) & 3
        return jnp.where(kind == 2, straight, jnp.where(kind == 3, crossed, zero))

    ups = []
    for j in range(16):
        children = jnp.concatenate([table[grand_ref[1 + z, j]] for z in range(4)], axis=1)
        up = dot_t(children, gt[grand_ref[0, j]])
        ups.append(jnp.where(grand_ref[5, j] == 1, up, 0.0).astype(BF16))
    grand_total = dot_t(jnp.concatenate(ups, axis=1), gc[0]).astype(BF16)
    down_two = dot(grand_total, gt[own_ref[0], :, pl.ds(pl.multiple_of(own_ref[1] * 128, 128), 128)])

    down_one = []
    for p in range(2):
        coefs = jnp.concatenate([pair_tile(parent_ref, p, 2 * i) for i in range(16)], axis=1)
        far = dot_t(coefs, pc[p])
        total = (far + down_two[:, p * 64 : (p + 1) * 64]).astype(BF16)
        down_one.append(dot(total, pt_ref[p]))

    for g in range(4):
        coefs = jnp.concatenate(
            [
                jnp.concatenate([pair_tile(leaf_ref, t, 2 * i) for i in range(16)], axis=1)
                for t in range(4 * g, 4 * g + 4)
            ],
            axis=0,
        )
        far = dot_t(coefs, lc[4 * g : 4 * g + 4].reshape(256, 2048))
        for k in range(4):
            t = 4 * g + k
            total = far[k * 16 : (k + 1) * 16, k * 64 : (k + 1) * 64]
            total = total + down_one[t // 8][:, (t % 8) * 64 : (t % 8 + 1) * 64]
            cols = slice(t * 256, (t + 1) * 256)
            here = slice((t % 8) * 256, (t % 8 + 1) * 256)
            near = jnp.where(second if t < 8 else first, near1_ref[:, here], near0_ref[:, here])
            out_ref[:, cols] = (dot(total.astype(BF16), basis_ref[t]) + near).astype(BF16)


def shift_plane(v, k, y_core):
    return lax.ppermute(
        v,
        AXES,
        pairs_of(
            lambda x, y, c, z: (x, (y + k) % 4, c, z) if c == y_core else ((x + k) % 4, y, c, z)
        ),
    )


def body(
    densities, basis, near_blocks, near_source, near_valid, leaf_coupling, leaf_source, leaf_valid,
    parent_transfer, parent_coupling, parent_source, parent_valid, grand_transfer, grand_coupling,
    grand_source, grand_valid,
):
    anywhere = pl.BlockSpec(memory_space=pl.ANY)
    vmem = pl.BlockSpec(memory_space=pltpu.VMEM)
    smem = pl.BlockSpec(memory_space=pltpu.SMEM)
    mz = lax.axis_index("z")
    own = jnp.stack([lax.axis_index(("x", "y", "c")), mz]).astype(jnp.int32)

    coefs, outer = pl.pallas_call(
        up_kernel,
        out_shape=[
            jax.ShapeDtypeStruct((TILES + 16, 16, 128), BF16),
            jax.ShapeDtypeStruct((16, 16, 128), BF16),
        ],
        in_specs=[anywhere] * 3,
        out_specs=[vmem] * 2,
        scratch_shapes=[
            pltpu.VMEM((16, 4096), BF16),
            pltpu.VMEM((16, 64, 256), BF16),
            pltpu.VMEM((2, 64, 512), BF16),
            pltpu.SemaphoreType.DMA((3,)),
        ],
        compiler_params=pltpu.CompilerParams(vmem_limit_bytes=UP_VMEM),
        name="upward",
    )(densities, basis, parent_transfer)

    barrier = lax.optimization_barrier
    swap = [(0, 1), (1, 0)]

    def near_half(turn, skip, halo, near_code):
        return pl.pallas_call(
            functools.partial(near_kernel, turn, skip),
            out_shape=jax.ShapeDtypeStruct((16, 2048), F32),
            in_specs=[smem, vmem, vmem, anywhere],
            out_specs=vmem,
            scratch_shapes=[
                pltpu.VMEM((33, 16, 256), BF16),
                pltpu.VMEM((8, 2048, 256), BF16),
                pltpu.SemaphoreType.DMA((8,)),
            ],
            compiler_params=pltpu.CompilerParams(vmem_limit_bytes=NEAR_VMEM),
            cost_estimate=pl.CostEstimate(
                flops=16 * 16 * 2048 * 256, bytes_accessed=8_700_000, transcendentals=0
            ),
            name="near",
        )(near_code, halo, tiles, near_blocks)

    coefs, densities, sources = barrier(
        (
            coefs,
            densities,
            (near_source.T, near_valid.T, leaf_source, leaf_valid, parent_source, parent_valid,
             grand_source, grand_valid),
        )
    )
    inner = lax.ppermute(coefs, "z", [(i, i ^ 1) for i in range(4)])
    mine = coefs[:TILES]
    steps = [lax.ppermute(mine, "z", [(i, i ^ k) for i in range(4)]) for k in (3, 2)]
    near_code, leaf_code, parent_code, grand_code = pl.pallas_call(
        code_kernel,
        out_shape=[
            jax.ShapeDtypeStruct(n, jnp.int32) for n in ((8, 16), (16, 32), (2, 32), (6, 16))
        ],
        compiler_params=pltpu.CompilerParams(vmem_limit_bytes=CODE_VMEM),
        name="codes",
    )(*sources)
    near_code, tiles = pl.pallas_call(
        stage_kernel,
        out_shape=[
            jax.ShapeDtypeStruct((8, 16), jnp.int32),
            jax.ShapeDtypeStruct((16, 16, 256), BF16),
        ],
        in_specs=[vmem] * 2,
        out_specs=[vmem] * 2,
        compiler_params=pltpu.CompilerParams(vmem_limit_bytes=STAGE_VMEM),
        name="stage",
    )(near_code, densities)
    coefs, inner, outer, near_code, tiles = barrier(
        (jnp.concatenate([mine, inner[:TILES]] + steps, axis=0), inner, outer, near_code, tiles)
    )

    outer = lax.ppermute(
        outer, AXES, [(i, i + 1) for i in range(1, 127, 2)] + [(i + 1, i) for i in range(1, 127, 2)]
    )

    steps = [shift_plane(coefs, k, 0) for k in (1, 2, 3)]
    near0 = near_half(0, TILES, inner, near_code)
    coefs, near0 = barrier((jnp.concatenate([coefs] + steps, axis=0), near0))

    first, second = coefs[:HALF], coefs[HALF:]
    ahead1, back2 = shift_plane(first, 1, 1), shift_plane(second, 3, 1)
    ahead2, back1 = shift_plane(second, 1, 1), shift_plane(first, 3, 1)
    ahead1, back2, near_code = barrier((ahead1, back2, near_code))
    far1, far2 = shift_plane(ahead1, 1, 1), shift_plane(back2, 3, 1)
    near1 = near_half(1, 0, outer, near_code)
    parts = [[coefs], [ahead1, back2], [ahead2, back1], [far1, far2]]
    other = [lax.ppermute(jnp.concatenate(p, axis=0), "c", swap) for p in parts]
    table = jnp.concatenate(sum(parts, []) + other, axis=0)

    return pl.pallas_call(
        down_kernel,
        out_shape=jax.ShapeDtypeStruct((16, 4096), BF16),
        in_specs=[smem] * 4 + [vmem] * 9,
        out_specs=vmem,
        compiler_params=pltpu.CompilerParams(vmem_limit_bytes=DOWN_VMEM),
        name="downward",
    )(
        leaf_code, parent_code, grand_code, own, table,
        leaf_coupling, parent_coupling, grand_coupling, grand_transfer, parent_transfer, basis,
        near0, near1,
    )


def solution(mesh):
    grid = Mesh(mesh.devices.reshape(4, 4, 2, 4), AXES)
    leaf, both = ("x", "y", "c"), AXES
    row, cube = P(both, None), P(both, None, None)
    return jax.shard_map(
        body,
        mesh=grid,
        in_specs=(
            P(None, both), cube, cube, row, row, cube, row, row, cube, cube, row, row, P(),
            P(leaf, None, None), P(leaf, None), P(leaf, None),
        ),
        out_specs=P(None, both),
        check_vma=False,
    )
```

```python
import functools

import jax
import jax.numpy as jnp
from jax import lax
from jax.experimental import pallas as pl
from jax.experimental.pallas import tpu as pltpu
from jax.sharding import Mesh, PartitionSpec as P

AXES = ("x", "y", "c", "z")
BF16, F32 = jnp.bfloat16, jnp.float32
TILES = 9
HALF = 8 * TILES
UP_VMEM, CODE_VMEM, STAGE_VMEM, NEAR_VMEM = 56_300_000, 65_000_000, 1 << 20, 40_000_000
AHEAD = 4
DOWN_VMEM = 20 * 1024 * 1024


def flat_index(x, y, c, z):
    return ((x * 4 + y) * 2 + c) * 4 + z


def pairs_of(move):
    return [
        (flat_index(x, y, c, z), flat_index(*move(x, y, c, z)))
        for x in range(4)
        for y in range(4)
        for c in range(2)
        for z in range(4)
    ]


def dot_t(a, b):
    return lax.dot_general(a, b, (((1,), (1,)), ((), ())), preferred_element_type=F32)


def dot(a, b):
    return lax.dot_general(a, b, (((1,), (0,)), ((), ())), preferred_element_type=F32)


def up_kernel(
    dens_hbm, basis_hbm, pt_hbm, out_ref, outer_ref, dens_ref, basis_ref, pt_ref, sems
):
    copies = [
        pltpu.make_async_copy(a, b, sems.at[k])
        for k, (a, b) in enumerate(
            ((dens_hbm, dens_ref), (basis_hbm, basis_ref), (pt_hbm, pt_ref))
        )
    ]
    for copy in copies:
        copy.start()
    for copy in copies:
        copy.wait()
    even = lax.axis_index("z") % 2 == 0
    for i in range(16):
        head, tail = (dens_ref[:, k * 128 : (k + 1) * 128] for k in (i, 16 + i))
        out_ref[TILES + i] = jnp.where(even, tail, head)
        outer_ref[i] = jnp.where(even, head, tail)
    tiles = []
    for i in range(8):
        pair = [
            dot_t(dens_ref[:, t * 256 : (t + 1) * 256], basis_ref[t]).astype(BF16)
            for t in (2 * i, 2 * i + 1)
        ]
        tile = jnp.concatenate(pair, axis=1)
        out_ref[i] = tile
        tiles.append(tile)
    pair = [
        dot_t(jnp.concatenate(tiles[4 * p : 4 * p + 4], axis=1), pt_ref[p]).astype(BF16)
        for p in range(2)
    ]
    out_ref[8] = jnp.concatenate(pair, axis=1)


def code_kernel(
    ns_ref, nv_ref, ls_ref, lv_ref, ps_ref, pv_ref, gs_ref, gv_ref,
    near_ref, leaf_ref, parent_ref, grand_ref,
):
    mx, my, mc, mz = (lax.axis_index(a) for a in AXES)
    me = flat_index(mx, my, mc, mz)

    def block_tile(device):
        z, c, y, x = device & 3, (device >> 2) & 1, (device >> 3) & 3, device >> 5
        w = z ^ mz
        kz = w ^ (w >> 1)
        ky, kx = (my - y) & 3, (mx - x) & 3
        near_step, far_step = jnp.where(c == 0, ky, kx), jnp.where(c == 0, kx, ky)
        half = near_step >> 1
        unit = jnp.where(far_step == 1, 2 + 2 * half, jnp.where(far_step == 3, 5 - 2 * half, 6 + half))
        unit = jnp.where(far_step == 0, half, unit) + jnp.where(c == mc, 0, 8)
        return unit * HALF + ((near_step & 1) * 4 + kz) * TILES

    def code(tile, source, valid):
        flip = (source + lax.broadcasted_iota(jnp.int32, source.shape, 1)) & 1
        return tile * 4 + valid * 2 + flip

    near_ref[...] = jnp.where(nv_ref[...] == 1, ns_ref[...] - (me * 16 - 8), 32)
    ls = ls_ref[...]
    leaf_ref[...] = code(block_tile(ls >> 4) + ((ls >> 1) & 7), ls, lv_ref[...])
    ps = ps_ref[...]
    parent_ref[...] = code(block_tile(ps >> 1) + 8, ps, pv_ref[...])
    gs = gs_ref[...]
    grand_ref[0:1] = gs
    for z in range(4):
        grand_ref[1 + z : 2 + z] = block_tile(gs * 4 + z) + 8
    grand_ref[5:6] = gv_ref[...]


def stage_kernel(code_ref, dens_ref, out_ref, tiles_ref):
    out_ref[...] = code_ref[...]
    for i in range(16):
        tiles_ref[i] = dens_ref[:, i * 256 : (i + 1) * 256]


def near_kernel(turn, skip, idx_ref, halo_ref, tiles_ref, blocks_hbm, out_ref, padded, blocks, sems):
    half = (lax.axis_index("z") + 1 + turn) & 1
    copies = [
        pltpu.make_async_copy(blocks_hbm.at[half * 8 + t], blocks.at[t], sems.at[t])
        for t in range(8)
    ]
    for copy in copies[:AHEAD]:
        copy.start()
    for i in range(8):
        pair = [halo_ref[skip + 2 * i + k] for k in range(2)]
        padded[24 * half + i] = jnp.concatenate(pair, axis=1)
    for i in range(16):
        padded[8 + i] = tiles_ref[i]
    padded[32] = jnp.zeros((16, 256), BF16)
    for t in range(8):
        if t + AHEAD < 8:
            copies[t + AHEAD].start()
        picked = jnp.concatenate([padded[idx_ref[j, half * 8 + t]] for j in range(8)], axis=1)
        copies[t].wait()
        out_ref[:, t * 256 : (t + 1) * 256] = dot(picked, blocks[t])


def down_kernel(
    leaf_ref, parent_ref, grand_ref, own_ref,
    table, lc, pc, gc, gt, pt_ref, basis_ref, near0_ref, near1_ref,
    out_ref,
):
    first = lax.axis_index("z") % 2 == 1
    second = jnp.logical_not(first)
    low = lax.broadcasted_iota(jnp.int32, (16, 128), 1) < 64
    zero = jnp.zeros((16, 128), BF16)

    def pair_tile(ref, t, j):
        first, second = ref[t, j], ref[t, j + 1]
        a, b = table[first >> 2], table[second >> 2]
        straight = jnp.where(low, a, b)
        crossed = pltpu.roll(jnp.where(low, b, a), 64, 1)
        kind = jnp.where(low, first, second) & 3
        return jnp.where(kind == 2, straight, jnp.where(kind == 3, crossed, zero))

    ups = []
    for j in range(16):
        children = jnp.concatenate([table[grand_ref[1 + z, j]] for z in range(4)], axis=1)
        up = dot_t(children, gt[grand_ref[0, j]])
        ups.append(jnp.where(grand_ref[5, j] == 1, up, 0.0).astype(BF16))
    grand_total = dot_t(jnp.concatenate(ups, axis=1), gc[0]).astype(BF16)
    down_two = dot(grand_total, gt[own_ref[0], :, pl.ds(pl.multiple_of(own_ref[1] * 128, 128), 128)])

    down_one = []
    for p in range(2):
        coefs = jnp.concatenate([pair_tile(parent_ref, p, 2 * i) for i in range(16)], axis=1)
        far = dot_t(coefs, pc[p])
        total = (far + down_two[:, p * 64 : (p + 1) * 64]).astype(BF16)
        down_one.append(dot(total, pt_ref[p]))

    for g in range(4):
        coefs = jnp.concatenate(
            [
                jnp.concatenate([pair_tile(leaf_ref, t, 2 * i) for i in range(16)], axis=1)
                for t in range(4 * g, 4 * g + 4)
            ],
            axis=0,
        )
        far = dot_t(coefs, lc[4 * g : 4 * g + 4].reshape(256, 2048))
        for k in range(4):
            t = 4 * g + k
            total = far[k * 16 : (k + 1) * 16, k * 64 : (k + 1) * 64]
            total = total + down_one[t // 8][:, (t % 8) * 64 : (t % 8 + 1) * 64]
            cols = slice(t * 256, (t + 1) * 256)
            here = slice((t % 8) * 256, (t % 8 + 1) * 256)
            near = jnp.where(second if t < 8 else first, near1_ref[:, here], near0_ref[:, here])
            out_ref[:, cols] = (dot(total.astype(BF16), basis_ref[t]) + near).astype(BF16)


def shift_plane(v, k, y_core):
    return lax.ppermute(
        v,
        AXES,
        pairs_of(
            lambda x, y, c, z: (x, (y + k) % 4, c, z) if c == y_core else ((x + k) % 4, y, c, z)
        ),
    )


def body(
    densities, basis, near_blocks, near_source, near_valid, leaf_coupling, leaf_source, leaf_valid,
    parent_transfer, parent_coupling, parent_source, parent_valid, grand_transfer, grand_coupling,
    grand_source, grand_valid,
):
    anywhere = pl.BlockSpec(memory_space=pl.ANY)
    vmem = pl.BlockSpec(memory_space=pltpu.VMEM)
    smem = pl.BlockSpec(memory_space=pltpu.SMEM)
    mz = lax.axis_index("z")
    own = jnp.stack([lax.axis_index(("x", "y", "c")), mz]).astype(jnp.int32)

    coefs, outer = pl.pallas_call(
        up_kernel,
        out_shape=[
            jax.ShapeDtypeStruct((TILES + 16, 16, 128), BF16),
            jax.ShapeDtypeStruct((16, 16, 128), BF16),
        ],
        in_specs=[anywhere] * 3,
        out_specs=[vmem] * 2,
        scratch_shapes=[
            pltpu.VMEM((16, 4096), BF16),
            pltpu.VMEM((16, 64, 256), BF16),
            pltpu.VMEM((2, 64, 512), BF16),
            pltpu.SemaphoreType.DMA((3,)),
        ],
        compiler_params=pltpu.CompilerParams(vmem_limit_bytes=UP_VMEM),
        name="upward",
    )(densities, basis, parent_transfer)

    barrier = lax.optimization_barrier
    swap = [(0, 1), (1, 0)]

    def near_half(turn, skip, halo, near_code):
        return pl.pallas_call(
            functools.partial(near_kernel, turn, skip),
            out_shape=jax.ShapeDtypeStruct((16, 2048), F32),
            in_specs=[smem, vmem, vmem, anywhere],
            out_specs=vmem,
            scratch_shapes=[
                pltpu.VMEM((33, 16, 256), BF16),
                pltpu.VMEM((8, 2048, 256), BF16),
                pltpu.SemaphoreType.DMA((8,)),
            ],
            compiler_params=pltpu.CompilerParams(vmem_limit_bytes=NEAR_VMEM),
            cost_estimate=pl.CostEstimate(
                flops=16 * 16 * 2048 * 256, bytes_accessed=8_700_000, transcendentals=0
            ),
            name="near",
        )(near_code, halo, tiles, near_blocks)

    coefs, densities, sources = barrier(
        (
            coefs,
            densities,
            (near_source.T, near_valid.T, leaf_source, leaf_valid, parent_source, parent_valid,
             grand_source, grand_valid),
        )
    )
    inner = lax.ppermute(coefs, "z", [(i, i ^ 1) for i in range(4)])
    mine = coefs[:TILES]
    steps = [lax.ppermute(mine, "z", [(i, i ^ k) for i in range(4)]) for k in (3, 2)]
    near_code, leaf_code, parent_code, grand_code = pl.pallas_call(
        code_kernel,
        out_shape=[
            jax.ShapeDtypeStruct(n, jnp.int32) for n in ((8, 16), (16, 32), (2, 32), (6, 16))
        ],
        compiler_params=pltpu.CompilerParams(vmem_limit_bytes=CODE_VMEM),
        name="codes",
    )(*sources)
    near_code, tiles = pl.pallas_call(
        stage_kernel,
        out_shape=[
            jax.ShapeDtypeStruct((8, 16), jnp.int32),
            jax.ShapeDtypeStruct((16, 16, 256), BF16),
        ],
        in_specs=[vmem] * 2,
        out_specs=[vmem] * 2,
        compiler_params=pltpu.CompilerParams(vmem_limit_bytes=STAGE_VMEM),
        name="stage",
    )(near_code, densities)
    coefs, inner, outer, near_code, tiles = barrier(
        (jnp.concatenate([mine, inner[:TILES]] + steps, axis=0), inner, outer, near_code, tiles)
    )

    outer = lax.ppermute(
        outer, AXES, [(i, i + 1) for i in range(1, 127, 2)] + [(i + 1, i) for i in range(1, 127, 2)]
    )

    steps = [shift_plane(coefs, k, 0) for k in (1, 2, 3)]
    near0 = near_half(0, TILES, inner, near_code)
    coefs, near0 = barrier((jnp.concatenate([coefs] + steps, axis=0), near0))

    first, second = coefs[:HALF], coefs[HALF:]
    ahead1, back2 = shift_plane(first, 1, 1), shift_plane(second, 3, 1)
    ahead2, back1 = shift_plane(second, 1, 1), shift_plane(first, 3, 1)
    ahead1, back2, near_code = barrier((ahead1, back2, near_code))
    far1, far2 = shift_plane(ahead1, 1, 1), shift_plane(back2, 3, 1)
    near1 = near_half(1, 0, outer, near_code)
    ahead2, back1, near1 = barrier((ahead2, back1, near1))
    parts = [[coefs], [ahead1, back2], [ahead2, back1], [far1, far2]]
    other = [lax.ppermute(jnp.concatenate(p, axis=0), "c", swap) for p in parts]
    table = jnp.concatenate(sum(parts, []) + other, axis=0)

    return pl.pallas_call(
        down_kernel,
        out_shape=jax.ShapeDtypeStruct((16, 4096), BF16),
        in_specs=[smem] * 4 + [vmem] * 9,
        out_specs=vmem,
        compiler_params=pltpu.CompilerParams(vmem_limit_bytes=DOWN_VMEM),
        name="downward",
    )(
        leaf_code, parent_code, grand_code, own, table,
        leaf_coupling, parent_coupling, grand_coupling, grand_transfer, parent_transfer, basis,
        near0, near1,
    )


def solution(mesh):
    grid = Mesh(mesh.devices.reshape(4, 4, 2, 4), AXES)
    leaf, both = ("x", "y", "c"), AXES
    row, cube = P(both, None), P(both, None, None)
    return jax.shard_map(
        body,
        mesh=grid,
        in_specs=(
            P(None, both), cube, cube, row, row, cube, row, row, cube, cube, row, row, P(),
            P(leaf, None, None), P(leaf, None), P(leaf, None),
        ),
        out_specs=P(None, both),
        check_vma=False,
    )
```

```python
import functools

import jax
import jax.numpy as jnp
from jax import lax
from jax.experimental import pallas as pl
from jax.experimental.pallas import tpu as pltpu
from jax.sharding import Mesh, PartitionSpec as P

AXES = ("x", "y", "c", "z")
BF16, F32 = jnp.bfloat16, jnp.float32
TILES = 9
HALF = 8 * TILES
UP_VMEM, CODE_VMEM, STAGE_VMEM, NEAR_VMEM = 56_300_000, 65_000_000, 1 << 20, 40_000_000
AHEAD = 4
DOWN_VMEM = 20 * 1024 * 1024


def flat_index(x, y, c, z):
    return ((x * 4 + y) * 2 + c) * 4 + z


def pairs_of(move):
    return [
        (flat_index(x, y, c, z), flat_index(*move(x, y, c, z)))
        for x in range(4)
        for y in range(4)
        for c in range(2)
        for z in range(4)
    ]


def dot_t(a, b):
    return lax.dot_general(a, b, (((1,), (1,)), ((), ())), preferred_element_type=F32)


def dot(a, b):
    return lax.dot_general(a, b, (((1,), (0,)), ((), ())), preferred_element_type=F32)


def up_kernel(
    dens_hbm, basis_hbm, pt_hbm, out_ref, outer_ref, dens_ref, basis_ref, pt_ref, sems
):
    copies = [
        pltpu.make_async_copy(a, b, sems.at[k])
        for k, (a, b) in enumerate(
            ((dens_hbm, dens_ref), (basis_hbm, basis_ref), (pt_hbm, pt_ref))
        )
    ]
    for copy in copies:
        copy.start()
    for copy in copies:
        copy.wait()
    even = lax.axis_index("z") % 2 == 0
    for i in range(16):
        head, tail = (dens_ref[:, k * 128 : (k + 1) * 128] for k in (i, 16 + i))
        out_ref[TILES + i] = jnp.where(even, tail, head)
        outer_ref[i] = jnp.where(even, head, tail)
    tiles = []
    for i in range(8):
        pair = [
            dot_t(dens_ref[:, t * 256 : (t + 1) * 256], basis_ref[t]).astype(BF16)
            for t in (2 * i, 2 * i + 1)
        ]
        tile = jnp.concatenate(pair, axis=1)
        out_ref[i] = tile
        tiles.append(tile)
    pair = [
        dot_t(jnp.concatenate(tiles[4 * p : 4 * p + 4], axis=1), pt_ref[p]).astype(BF16)
        for p in range(2)
    ]
    out_ref[8] = jnp.concatenate(pair, axis=1)


def code_kernel(
    ns_ref, nv_ref, ls_ref, lv_ref, ps_ref, pv_ref, gs_ref, gv_ref,
    near_ref, leaf_ref, parent_ref, grand_ref,
):
    mx, my, mc, mz = (lax.axis_index(a) for a in AXES)
    me = flat_index(mx, my, mc, mz)

    def block_tile(device):
        z, c, y, x = device & 3, (device >> 2) & 1, (device >> 3) & 3, device >> 5
        w = z ^ mz
        kz = w ^ (w >> 1)
        ky, kx = (my - y) & 3, (mx - x) & 3
        near_step, far_step = jnp.where(c == 0, ky, kx), jnp.where(c == 0, kx, ky)
        half = near_step >> 1
        unit = jnp.where(far_step == 1, 2 + 2 * half, jnp.where(far_step == 3, 5 - 2 * half, 6 + half))
        unit = jnp.where(far_step == 0, half, unit) + jnp.where(c == mc, 0, 8)
        return unit * HALF + ((near_step & 1) * 4 + kz) * TILES

    def code(tile, source, valid):
        flip = (source + lax.broadcasted_iota(jnp.int32, source.shape, 1)) & 1
        return tile * 4 + valid * 2 + flip

    near_ref[...] = jnp.where(nv_ref[...] == 1, ns_ref[...] - (me * 16 - 8), 32)
    ls = ls_ref[...]
    leaf_ref[...] = code(block_tile(ls >> 4) + ((ls >> 1) & 7), ls, lv_ref[...])
    ps = ps_ref[...]
    parent_ref[...] = code(block_tile(ps >> 1) + 8, ps, pv_ref[...])
    gs = gs_ref[...]
    grand_ref[0:1] = gs
    for z in range(4):
        grand_ref[1 + z : 2 + z] = block_tile(gs * 4 + z) + 8
    grand_ref[5:6] = gv_ref[...]


def stage_kernel(code_ref, dens_ref, out_ref, tiles_ref):
    out_ref[...] = code_ref[...]
    for i in range(16):
        tiles_ref[i] = dens_ref[:, i * 256 : (i + 1) * 256]


def near_kernel(turn, skip, idx_ref, halo_ref, tiles_ref, blocks_hbm, out_ref, padded, blocks, sems):
    half = (lax.axis_index("z") + 1 + turn) & 1
    copies = [
        pltpu.make_async_copy(blocks_hbm.at[half * 8 + t], blocks.at[t], sems.at[t])
        for t in range(8)
    ]
    for copy in copies[:AHEAD]:
        copy.start()
    for i in range(8):
        pair = [halo_ref[skip + 2 * i + k] for k in range(2)]
        padded[24 * half + i] = jnp.concatenate(pair, axis=1)
    for i in range(16):
        padded[8 + i] = tiles_ref[i]
    padded[32] = jnp.zeros((16, 256), BF16)
    for t in range(8):
        if t + AHEAD < 8:
            copies[t + AHEAD].start()
        picked = jnp.concatenate([padded[idx_ref[j, half * 8 + t]] for j in range(8)], axis=1)
        copies[t].wait()
        out_ref[:, t * 256 : (t + 1) * 256] = dot(picked, blocks[t])


def down_kernel(
    leaf_ref, parent_ref, grand_ref, own_ref,
    table, lc, pc, gc, gt, pt_ref, basis_ref, near0_ref, near1_ref,
    out_ref,
):
    first = lax.axis_index("z") % 2 == 1
    second = jnp.logical_not(first)
    low = lax.broadcasted_iota(jnp.int32, (16, 128), 1) < 64
    zero = jnp.zeros((16, 128), BF16)

    def pair_tile(ref, t, j):
        first, second = ref[t, j], ref[t, j + 1]
        a, b = table[first >> 2], table[second >> 2]
        straight = jnp.where(low, a, b)
        crossed = pltpu.roll(jnp.where(low, b, a), 64, 1)
        kind = jnp.where(low, first, second) & 3
        return jnp.where(kind == 2, straight, jnp.where(kind == 3, crossed, zero))

    fars = []
    for g in range(4):
        coefs = jnp.concatenate(
            [
                jnp.concatenate([pair_tile(leaf_ref, t, 2 * i) for i in range(16)], axis=1)
                for t in range(4 * g, 4 * g + 4)
            ],
            axis=0,
        )
        fars.append(dot_t(coefs, lc[4 * g : 4 * g + 4].reshape(256, 2048)))

    ups = []
    for j in range(16):
        children = jnp.concatenate([table[grand_ref[1 + z, j]] for z in range(4)], axis=1)
        up = dot_t(children, gt[grand_ref[0, j]])
        ups.append(jnp.where(grand_ref[5, j] == 1, up, 0.0).astype(BF16))
    grand_total = dot_t(jnp.concatenate(ups, axis=1), gc[0]).astype(BF16)
    down_two = dot(grand_total, gt[own_ref[0], :, pl.ds(pl.multiple_of(own_ref[1] * 128, 128), 128)])

    down_one = []
    for p in range(2):
        coefs = jnp.concatenate([pair_tile(parent_ref, p, 2 * i) for i in range(16)], axis=1)
        far = dot_t(coefs, pc[p])
        total = (far + down_two[:, p * 64 : (p + 1) * 64]).astype(BF16)
        down_one.append(dot(total, pt_ref[p]))

    for g in range(4):
        far = fars[g]
        for k in range(4):
            t = 4 * g + k
            total = far[k * 16 : (k + 1) * 16, k * 64 : (k + 1) * 64]
            total = total + down_one[t // 8][:, (t % 8) * 64 : (t % 8 + 1) * 64]
            cols = slice(t * 256, (t + 1) * 256)
            here = slice((t % 8) * 256, (t % 8 + 1) * 256)
            near = jnp.where(second if t < 8 else first, near1_ref[:, here], near0_ref[:, here])
            out_ref[:, cols] = (dot(total.astype(BF16), basis_ref[t]) + near).astype(BF16)


def shift_plane(v, k, y_core):
    return lax.ppermute(
        v,
        AXES,
        pairs_of(
            lambda x, y, c, z: (x, (y + k) % 4, c, z) if c == y_core else ((x + k) % 4, y, c, z)
        ),
    )


def body(
    densities, basis, near_blocks, near_source, near_valid, leaf_coupling, leaf_source, leaf_valid,
    parent_transfer, parent_coupling, parent_source, parent_valid, grand_transfer, grand_coupling,
    grand_source, grand_valid,
):
    anywhere = pl.BlockSpec(memory_space=pl.ANY)
    vmem = pl.BlockSpec(memory_space=pltpu.VMEM)
    smem = pl.BlockSpec(memory_space=pltpu.SMEM)
    mz = lax.axis_index("z")
    own = jnp.stack([lax.axis_index(("x", "y", "c")), mz]).astype(jnp.int32)

    coefs, outer = pl.pallas_call(
        up_kernel,
        out_shape=[
            jax.ShapeDtypeStruct((TILES + 16, 16, 128), BF16),
            jax.ShapeDtypeStruct((16, 16, 128), BF16),
        ],
        in_specs=[anywhere] * 3,
        out_specs=[vmem] * 2,
        scratch_shapes=[
            pltpu.VMEM((16, 4096), BF16),
            pltpu.VMEM((16, 64, 256), BF16),
            pltpu.VMEM((2, 64, 512), BF16),
            pltpu.SemaphoreType.DMA((3,)),
        ],
        compiler_params=pltpu.CompilerParams(vmem_limit_bytes=UP_VMEM),
        name="upward",
    )(densities, basis, parent_transfer)

    barrier = lax.optimization_barrier
    swap = [(0, 1), (1, 0)]

    def near_half(turn, skip, halo, near_code):
        return pl.pallas_call(
            functools.partial(near_kernel, turn, skip),
            out_shape=jax.ShapeDtypeStruct((16, 2048), F32),
            in_specs=[smem, vmem, vmem, anywhere],
            out_specs=vmem,
            scratch_shapes=[
                pltpu.VMEM((33, 16, 256), BF16),
                pltpu.VMEM((8, 2048, 256), BF16),
                pltpu.SemaphoreType.DMA((8,)),
            ],
            compiler_params=pltpu.CompilerParams(vmem_limit_bytes=NEAR_VMEM),
            cost_estimate=pl.CostEstimate(
                flops=16 * 16 * 2048 * 256, bytes_accessed=8_700_000, transcendentals=0
            ),
            name="near",
        )(near_code, halo, tiles, near_blocks)

    coefs, densities, sources = barrier(
        (
            coefs,
            densities,
            (near_source.T, near_valid.T, leaf_source, leaf_valid, parent_source, parent_valid,
             grand_source, grand_valid),
        )
    )
    inner = lax.ppermute(coefs, "z", [(i, i ^ 1) for i in range(4)])
    mine = coefs[:TILES]
    steps = [lax.ppermute(mine, "z", [(i, i ^ k) for i in range(4)]) for k in (3, 2)]
    near_code, leaf_code, parent_code, grand_code = pl.pallas_call(
        code_kernel,
        out_shape=[
            jax.ShapeDtypeStruct(n, jnp.int32) for n in ((8, 16), (16, 32), (2, 32), (6, 16))
        ],
        compiler_params=pltpu.CompilerParams(vmem_limit_bytes=CODE_VMEM),
        name="codes",
    )(*sources)
    near_code, tiles = pl.pallas_call(
        stage_kernel,
        out_shape=[
            jax.ShapeDtypeStruct((8, 16), jnp.int32),
            jax.ShapeDtypeStruct((16, 16, 256), BF16),
        ],
        in_specs=[vmem] * 2,
        out_specs=[vmem] * 2,
        compiler_params=pltpu.CompilerParams(vmem_limit_bytes=STAGE_VMEM),
        name="stage",
    )(near_code, densities)
    coefs, inner, outer, near_code, tiles = barrier(
        (jnp.concatenate([mine, inner[:TILES]] + steps, axis=0), inner, outer, near_code, tiles)
    )

    outer = lax.ppermute(
        outer, AXES, [(i, i + 1) for i in range(1, 127, 2)] + [(i + 1, i) for i in range(1, 127, 2)]
    )

    steps = [shift_plane(coefs, k, 0) for k in (1, 2, 3)]
    near0 = near_half(0, TILES, inner, near_code)
    coefs, near0 = barrier((jnp.concatenate([coefs] + steps, axis=0), near0))
    own_swap = lax.ppermute(coefs, "c", swap)

    first, second = coefs[:HALF], coefs[HALF:]
    ahead1, back2 = shift_plane(first, 1, 1), shift_plane(second, 3, 1)
    ahead2, back1 = shift_plane(second, 1, 1), shift_plane(first, 3, 1)
    ahead1, back2, near_code, own_swap = barrier((ahead1, back2, near_code, own_swap))
    far1, far2 = shift_plane(ahead1, 1, 1), shift_plane(back2, 3, 1)
    near1 = near_half(1, 0, outer, near_code)
    ahead2, back1, near1 = barrier((ahead2, back1, near1))
    parts = [[coefs], [ahead1, back2], [ahead2, back1], [far1, far2]]
    other = [own_swap] + [lax.ppermute(jnp.concatenate(p, axis=0), "c", swap) for p in parts[1:]]
    table = jnp.concatenate(sum(parts, []) + other, axis=0)

    return pl.pallas_call(
        down_kernel,
        out_shape=jax.ShapeDtypeStruct((16, 4096), BF16),
        in_specs=[smem] * 4 + [vmem] * 9,
        out_specs=vmem,
        compiler_params=pltpu.CompilerParams(vmem_limit_bytes=DOWN_VMEM),
        name="downward",
    )(
        leaf_code, parent_code, grand_code, own, table,
        leaf_coupling, parent_coupling, grand_coupling, grand_transfer, parent_transfer, basis,
        near0, near1,
    )


def solution(mesh):
    grid = Mesh(mesh.devices.reshape(4, 4, 2, 4), AXES)
    leaf, both = ("x", "y", "c"), AXES
    row, cube = P(both, None), P(both, None, None)
    return jax.shard_map(
        body,
        mesh=grid,
        in_specs=(
            P(None, both), cube, cube, row, row, cube, row, row, cube, cube, row, row, P(),
            P(leaf, None, None), P(leaf, None), P(leaf, None),
        ),
        out_specs=P(None, both),
        check_vma=False,
    )
```

```python
import functools

import jax
import jax.numpy as jnp
from jax import lax
from jax.experimental import pallas as pl
from jax.experimental.pallas import tpu as pltpu
from jax.sharding import Mesh, PartitionSpec as P

AXES = ("x", "y", "c", "z")
BF16, F32 = jnp.bfloat16, jnp.float32
TILES = 9
HALF = 8 * TILES
UP_VMEM, CODE_VMEM, STAGE_VMEM, NEAR_VMEM = 56_300_000, 65_000_000, 1 << 20, 40_000_000
AHEAD = 4
DOWN_VMEM = 20 * 1024 * 1024


def flat_index(x, y, c, z):
    return ((x * 4 + y) * 2 + c) * 4 + z


def pairs_of(move):
    return [
        (flat_index(x, y, c, z), flat_index(*move(x, y, c, z)))
        for x in range(4)
        for y in range(4)
        for c in range(2)
        for z in range(4)
    ]


def dot_t(a, b):
    return lax.dot_general(a, b, (((1,), (1,)), ((), ())), preferred_element_type=F32)


def dot(a, b):
    return lax.dot_general(a, b, (((1,), (0,)), ((), ())), preferred_element_type=F32)


def up_kernel(
    dens_hbm, basis_hbm, pt_hbm, out_ref, outer_ref, dens_ref, basis_ref, pt_ref, sems
):
    copies = [
        pltpu.make_async_copy(a, b, sems.at[k])
        for k, (a, b) in enumerate(
            ((dens_hbm, dens_ref), (basis_hbm, basis_ref), (pt_hbm, pt_ref))
        )
    ]
    for copy in copies:
        copy.start()
    for copy in copies:
        copy.wait()
    even = lax.axis_index("z") % 2 == 0
    for i in range(16):
        head, tail = (dens_ref[:, k * 128 : (k + 1) * 128] for k in (i, 16 + i))
        out_ref[TILES + i] = jnp.where(even, tail, head)
        outer_ref[i] = jnp.where(even, head, tail)
    tiles = []
    for i in range(8):
        pair = [
            dot_t(dens_ref[:, t * 256 : (t + 1) * 256], basis_ref[t]).astype(BF16)
            for t in (2 * i, 2 * i + 1)
        ]
        tile = jnp.concatenate(pair, axis=1)
        out_ref[i] = tile
        tiles.append(tile)
    pair = [
        dot_t(jnp.concatenate(tiles[4 * p : 4 * p + 4], axis=1), pt_ref[p]).astype(BF16)
        for p in range(2)
    ]
    out_ref[8] = jnp.concatenate(pair, axis=1)


def code_kernel(
    ns_ref, nv_ref, ls_ref, lv_ref, ps_ref, pv_ref, gs_ref, gv_ref,
    near_ref, leaf_ref, parent_ref, grand_ref,
):
    mx, my, mc, mz = (lax.axis_index(a) for a in AXES)
    me = flat_index(mx, my, mc, mz)

    def block_tile(device):
        z, c, y, x = device & 3, (device >> 2) & 1, (device >> 3) & 3, device >> 5
        w = z ^ mz
        kz = w ^ (w >> 1)
        ky, kx = (my - y) & 3, (mx - x) & 3
        near_step, far_step = jnp.where(c == 0, ky, kx), jnp.where(c == 0, kx, ky)
        half = near_step >> 1
        unit = jnp.where(far_step == 1, 2 + 2 * half, jnp.where(far_step == 3, 5 - 2 * half, 6 + half))
        unit = jnp.where(far_step == 0, half, unit) + jnp.where(c == mc, 0, 8)
        return unit * HALF + ((near_step & 1) * 4 + kz) * TILES

    def code(tile, source, valid):
        flip = (source + lax.broadcasted_iota(jnp.int32, source.shape, 1)) & 1
        return tile * 4 + valid * 2 + flip

    near_ref[...] = jnp.where(nv_ref[...] == 1, ns_ref[...] - (me * 16 - 8), 32)
    ls = ls_ref[...]
    leaf_ref[...] = code(block_tile(ls >> 4) + ((ls >> 1) & 7), ls, lv_ref[...])
    ps = ps_ref[...]
    parent_ref[...] = code(block_tile(ps >> 1) + 8, ps, pv_ref[...])
    gs = gs_ref[...]
    grand_ref[0:1] = gs
    for z in range(4):
        grand_ref[1 + z : 2 + z] = block_tile(gs * 4 + z) + 8
    grand_ref[5:6] = gv_ref[...]


def stage_kernel(code_ref, dens_ref, out_ref, tiles_ref):
    out_ref[...] = code_ref[...]
    for i in range(16):
        tiles_ref[i] = dens_ref[:, i * 256 : (i + 1) * 256]


def near_kernel(turn, skip, idx_ref, halo_ref, tiles_ref, blocks_hbm, out_ref, padded, blocks, sems):
    half = (lax.axis_index("z") + 1 + turn) & 1
    copies = [
        pltpu.make_async_copy(blocks_hbm.at[half * 8 + t], blocks.at[t], sems.at[t])
        for t in range(8)
    ]
    for copy in copies[:AHEAD]:
        copy.start()
    for i in range(8):
        pair = [halo_ref[skip + 2 * i + k] for k in range(2)]
        padded[24 * half + i] = jnp.concatenate(pair, axis=1)
    for i in range(16):
        padded[8 + i] = tiles_ref[i]
    padded[32] = jnp.zeros((16, 256), BF16)
    for t in range(8):
        if t + AHEAD < 8:
            copies[t + AHEAD].start()
        picked = jnp.concatenate([padded[idx_ref[j, half * 8 + t]] for j in range(8)], axis=1)
        copies[t].wait()
        out_ref[:, t * 256 : (t + 1) * 256] = dot(picked, blocks[t])


def down_kernel(
    leaf_ref, parent_ref, grand_ref, own_ref,
    table, lc, pc, gc, gt, pt_ref, basis_ref, near0_ref, near1_ref,
    out_ref,
):
    first = lax.axis_index("z") % 2 == 1
    second = jnp.logical_not(first)
    low = lax.broadcasted_iota(jnp.int32, (16, 128), 1) < 64
    zero = jnp.zeros((16, 128), BF16)

    def pair_tile(ref, t, j):
        first, second = ref[t, j], ref[t, j + 1]
        a, b = table[first >> 2], table[second >> 2]
        straight = jnp.where(low, a, b)
        crossed = pltpu.roll(jnp.where(low, b, a), 64, 1)
        kind = jnp.where(low, first, second) & 3
        return jnp.where(kind == 2, straight, jnp.where(kind == 3, crossed, zero))

    fars = []
    for g in range(4):
        coefs = jnp.concatenate(
            [
                jnp.concatenate([pair_tile(leaf_ref, t, 2 * i) for i in range(16)], axis=1)
                for t in range(4 * g, 4 * g + 4)
            ],
            axis=0,
        )
        fars.append(dot_t(coefs, lc[4 * g : 4 * g + 4].reshape(256, 2048)))

    ups = []
    for j in range(16):
        children = jnp.concatenate([table[grand_ref[1 + z, j]] for z in range(4)], axis=1)
        up = dot_t(children, gt[grand_ref[0, j]])
        ups.append(jnp.where(grand_ref[5, j] == 1, up, 0.0).astype(BF16))
    grand_total = dot_t(jnp.concatenate(ups, axis=1), gc[0]).astype(BF16)
    down_two = dot(grand_total, gt[own_ref[0], :, pl.ds(pl.multiple_of(own_ref[1] * 128, 128), 128)])

    down_one = []
    for p in range(2):
        coefs = jnp.concatenate([pair_tile(parent_ref, p, 2 * i) for i in range(16)], axis=1)
        far = dot_t(coefs, pc[p])
        total = (far + down_two[:, p * 64 : (p + 1) * 64]).astype(BF16)
        down_one.append(dot(total, pt_ref[p]))

    for g in range(4):
        far = fars[g]
        for k in range(4):
            t = 4 * g + k
            total = far[k * 16 : (k + 1) * 16, k * 64 : (k + 1) * 64]
            total = total + down_one[t // 8][:, (t % 8) * 64 : (t % 8 + 1) * 64]
            cols = slice(t * 256, (t + 1) * 256)
            here = slice((t % 8) * 256, (t % 8 + 1) * 256)
            near = jnp.where(second if t < 8 else first, near1_ref[:, here], near0_ref[:, here])
            out_ref[:, cols] = (dot(total.astype(BF16), basis_ref[t]) + near).astype(BF16)


def shift_plane(v, k, y_core):
    return lax.ppermute(
        v,
        AXES,
        pairs_of(
            lambda x, y, c, z: (x, (y + k) % 4, c, z) if c == y_core else ((x + k) % 4, y, c, z)
        ),
    )


def body(
    densities, basis, near_blocks, near_source, near_valid, leaf_coupling, leaf_source, leaf_valid,
    parent_transfer, parent_coupling, parent_source, parent_valid, grand_transfer, grand_coupling,
    grand_source, grand_valid,
):
    anywhere = pl.BlockSpec(memory_space=pl.ANY)
    vmem = pl.BlockSpec(memory_space=pltpu.VMEM)
    smem = pl.BlockSpec(memory_space=pltpu.SMEM)
    mz = lax.axis_index("z")
    own = jnp.stack([lax.axis_index(("x", "y", "c")), mz]).astype(jnp.int32)

    coefs, outer = pl.pallas_call(
        up_kernel,
        out_shape=[
            jax.ShapeDtypeStruct((TILES + 16, 16, 128), BF16),
            jax.ShapeDtypeStruct((16, 16, 128), BF16),
        ],
        in_specs=[anywhere] * 3,
        out_specs=[vmem] * 2,
        scratch_shapes=[
            pltpu.VMEM((16, 4096), BF16),
            pltpu.VMEM((16, 64, 256), BF16),
            pltpu.VMEM((2, 64, 512), BF16),
            pltpu.SemaphoreType.DMA((3,)),
        ],
        compiler_params=pltpu.CompilerParams(vmem_limit_bytes=UP_VMEM),
        name="upward",
    )(densities, basis, parent_transfer)

    barrier = lax.optimization_barrier
    swap = [(0, 1), (1, 0)]

    def near_half(turn, skip, halo, near_code):
        return pl.pallas_call(
            functools.partial(near_kernel, turn, skip),
            out_shape=jax.ShapeDtypeStruct((16, 2048), F32),
            in_specs=[smem, vmem, vmem, anywhere],
            out_specs=vmem,
            scratch_shapes=[
                pltpu.VMEM((33, 16, 256), BF16),
                pltpu.VMEM((8, 2048, 256), BF16),
                pltpu.SemaphoreType.DMA((8,)),
            ],
            compiler_params=pltpu.CompilerParams(vmem_limit_bytes=NEAR_VMEM),
            cost_estimate=pl.CostEstimate(
                flops=16 * 16 * 2048 * 256, bytes_accessed=8_700_000, transcendentals=0
            ),
            name="near",
        )(near_code, halo, tiles, near_blocks)

    coefs, densities, sources = barrier(
        (
            coefs,
            densities,
            (near_source.T, near_valid.T, leaf_source, leaf_valid, parent_source, parent_valid,
             grand_source, grand_valid),
        )
    )
    mine = coefs[:TILES]
    opposite = lax.ppermute(mine, "z", [(i, i ^ 2) for i in range(4)])
    inner = lax.ppermute(coefs, "z", [(i, i ^ 1) for i in range(4)])
    steps = [lax.ppermute(mine, "z", [(i, i ^ 3) for i in range(4)]), opposite]
    near_code, leaf_code, parent_code, grand_code = pl.pallas_call(
        code_kernel,
        out_shape=[
            jax.ShapeDtypeStruct(n, jnp.int32) for n in ((8, 16), (16, 32), (2, 32), (6, 16))
        ],
        compiler_params=pltpu.CompilerParams(vmem_limit_bytes=CODE_VMEM),
        name="codes",
    )(*sources)
    near_code, tiles = pl.pallas_call(
        stage_kernel,
        out_shape=[
            jax.ShapeDtypeStruct((8, 16), jnp.int32),
            jax.ShapeDtypeStruct((16, 16, 256), BF16),
        ],
        in_specs=[vmem] * 2,
        out_specs=[vmem] * 2,
        compiler_params=pltpu.CompilerParams(vmem_limit_bytes=STAGE_VMEM),
        name="stage",
    )(near_code, densities)
    coefs, inner, outer, near_code, tiles = barrier(
        (jnp.concatenate([mine, inner[:TILES]] + steps, axis=0), inner, outer, near_code, tiles)
    )

    outer = lax.ppermute(
        outer, AXES, [(i, i + 1) for i in range(1, 127, 2)] + [(i + 1, i) for i in range(1, 127, 2)]
    )

    opposite = shift_plane(coefs, 2, 0)
    steps = [shift_plane(coefs, 1, 0), opposite, shift_plane(coefs, 3, 0)]
    near0 = near_half(0, TILES, inner, near_code)
    coefs, near0 = barrier((jnp.concatenate([coefs] + steps, axis=0), near0))
    own_swap = lax.ppermute(coefs, "c", swap)

    first, second = coefs[:HALF], coefs[HALF:]
    ahead1, back2 = shift_plane(first, 1, 1), shift_plane(second, 3, 1)
    ahead2, back1 = shift_plane(second, 1, 1), shift_plane(first, 3, 1)
    ahead1, back2, near_code, own_swap = barrier((ahead1, back2, near_code, own_swap))
    far1, far2 = shift_plane(ahead1, 1, 1), shift_plane(back2, 3, 1)
    near1 = near_half(1, 0, outer, near_code)
    ahead2, back1, near1 = barrier((ahead2, back1, near1))
    parts = [[coefs], [ahead1, back2], [ahead2, back1], [far1, far2]]
    other = [own_swap] + [lax.ppermute(jnp.concatenate(p, axis=0), "c", swap) for p in parts[1:]]
    table = jnp.concatenate(sum(parts, []) + other, axis=0)

    return pl.pallas_call(
        down_kernel,
        out_shape=jax.ShapeDtypeStruct((16, 4096), BF16),
        in_specs=[smem] * 4 + [vmem] * 9,
        out_specs=vmem,
        compiler_params=pltpu.CompilerParams(vmem_limit_bytes=DOWN_VMEM),
        name="downward",
    )(
        leaf_code, parent_code, grand_code, own, table,
        leaf_coupling, parent_coupling, grand_coupling, grand_transfer, parent_transfer, basis,
        near0, near1,
    )


def solution(mesh):
    grid = Mesh(mesh.devices.reshape(4, 4, 2, 4), AXES)
    leaf, both = ("x", "y", "c"), AXES
    row, cube = P(both, None), P(both, None, None)
    return jax.shard_map(
        body,
        mesh=grid,
        in_specs=(
            P(None, both), cube, cube, row, row, cube, row, row, cube, cube, row, row, P(),
            P(leaf, None, None), P(leaf, None), P(leaf, None),
        ),
        out_specs=P(None, both),
        check_vma=False,
    )
```
